32 devices in a mesh: gx: 8 (over z, y), yz: 4 (over x, core).
Axes of the slice: x: 2, y: 2, z: 4, core: 2. Of those that a mesh axis runs over, the one named last changes fastest.
Arguments:
- mean_mix: float32 [131072], P(('gx', 'yz')), may hold values from 0.05 to 0.95
- segregation: float32 [131072], P(('gx', 'yz')), may hold values from 0.012 to 0.3
- dissipation: float32 [131072], P(('gx', 'yz')), may hold values from 0.04 to 0.4
- les_map: int32 [131072], P(('gx', 'yz')), may hold values from 0 to 255
- cond_state: float32 [10, 64, 8192], P(None, None, ('gx', 'yz')), may hold values from -6 to 6
- slot_cell: int32 [8192], P(('gx', 'yz')), may hold values from 0 to 8191, as said below
- adjacency: int32 [4, 8192], P(None, ('gx', 'yz')), may hold values from 0 to 383
- substeps: int32 [8192], P(('gx', 'yz')), may hold values from 1 to 8
- coupling: float32 [10, 10], replicated, may hold values from -2 to 2
Outputs:
- species: float32 [10, 131072], P(None, ('gx', 'yz'))
- cond_new: float32 [10, 64, 8192], P(None, None, ('gx', 'yz'))
The draws below stay inside these ranges and needn't reach their ends.
Inputs may be any that keep to these rules, and one draw needn't show every extreme that they name: `slot_cell`: A permutation of the CMC cells. The 256 slots of each device hold exactly 16 cells of each of half of the tiles and none of the others; each tile's cells lie on half of the devices, exactly 16 on each.
All inputs are finite; a program needn't handle non-finite values.
Results may differ from the reference program's by a relative error of at most 0.00018.
Values sent between devices are 32-bit elements; how exact they have to be, the bound alone decides.
A program may use at most 64 MiB of HBM per device.

```python
import math
import jax
import jax.numpy as jnp
from jax import lax

K = 10
B = 64
SUBMAX = 8
CMC_DEV = 256
LES_DEV = 4096
RIM = 32
NCMC = 8192
NLES = 131072
N_GX = 8
N_YZ = 4


def slot_layout(key):
    cells = CMC_DEV
    devices = NCMC // CMC_DEV
    half_dev = devices // 2
    slot_cap = 2 * cells // devices
    key_shift, key_cell, key_slot = jax.random.split(jax.random.fold_in(key, 17), 3)
    candidates = jnp.arange(devices - 2, dtype=jnp.int32)
    others = jnp.where(candidates == 0, 0, candidates + 1)
    picked = jax.random.permutation(key_shift, others)[:half_dev - 2].astype(jnp.int32)
    shifts = jnp.concatenate([jnp.array([1, devices - 1], jnp.int32), picked])
    cell_order = jax.vmap(lambda one_key: jax.random.permutation(one_key, cells))(jax.random.split(key_cell, devices)).astype(jnp.int32)
    slot_order = jax.vmap(lambda one_key: jax.random.permutation(one_key, cells))(jax.random.split(key_slot, devices)).astype(jnp.int32)
    group_id = cell_order // slot_cap
    within = cell_order % slot_cap
    tile_ids = jnp.arange(devices, dtype=jnp.int32)[:, None]
    owner = (tile_ids + shifts[group_id]) % devices
    local_slot = slot_order[owner, group_id * slot_cap + within]
    slot_id = owner * cells + local_slot
    geometric = tile_ids * cells + jnp.arange(cells, dtype=jnp.int32)[None, :]
    return jnp.zeros((devices * cells,), jnp.int32).at[slot_id.reshape(-1)].set(geometric.reshape(-1))


def draw_slot_cell(key, part):
    return slot_layout(key)


def draw_substeps(key, part):
    cells = CMC_DEV
    devices = NCMC // CMC_DEV
    slot_now = slot_layout(key)
    tile_now = slot_now // cells
    local_now = slot_now % cells
    key_hot, key_high, key_low = jax.random.split(jax.random.fold_in(key, 29), 3)
    hot_count = max(1, devices // 8)
    hot_tiles = jax.random.permutation(key_hot, devices)[:hot_count].astype(jnp.int32)
    is_hot = jnp.any(tile_now[:, None] == hot_tiles[None, :], axis=1)
    high_val = jax.random.randint(key_high, (NCMC,), SUBMAX // 2, SUBMAX + 1)
    low_val = jax.random.randint(key_low, (NCMC,), 1, 3)
    high_val = jnp.where(local_now == 0, SUBMAX, high_val)
    low_val = jnp.where(local_now == 1, 1, low_val)
    return jnp.where(is_hot, high_val, low_val).astype(jnp.int32)


def draw_cond_state(key, part):
    key = jax.random.fold_in(key, 41)
    key_sign, key_noise = jax.random.split(key, 2)
    signs = jnp.where(jax.random.bernoulli(key_sign, 0.5, (K, B, NCMC)), 1.0, -1.0).astype(jnp.float32)
    values = 4.5 * signs + 0.5 * jax.random.normal(key_noise, (K, B, NCMC), jnp.float32)
    return jnp.clip(values, -6.0, 6.0).astype(jnp.float32)


def draw_segregation(key, part):
    key = jax.random.fold_in(key, 53)
    key_tiles, key_value = jax.random.split(key, 2)
    tiles = NLES // LES_DEV
    order = jax.random.permutation(key_tiles, tiles)
    narrow_tile = order < tiles // 2
    narrow = jnp.repeat(narrow_tile, LES_DEV)
    spread = jax.random.uniform(key_value, (NLES,), jnp.float32, 0.0, 1.0)
    broad = 0.02 + 0.28 * spread
    tight = 0.012 + 0.002 * spread
    return jnp.where(narrow, tight, broad).astype(jnp.float32)


def with_ends(drawn, stream_key, least, largest):
    dims = drawn.shape
    place = [jax.random.randint(jax.random.fold_in(stream_key, axis), (), 0, dims[axis]) for axis in range(len(dims))]
    drawn = drawn.at[tuple(place)].set(least)
    longest = dims.index(max(dims))
    place[longest] = (place[longest] + 1) % dims[longest]
    return drawn.at[tuple(place)].set(largest)


def block_levels(rng, extent, cuts, smallest, high):
    level, own = 1.0, jax.random.fold_in(rng, 6)
    for dim, shards_of in cuts:
        draws = jnp.exp(jax.random.uniform(jax.random.fold_in(own, dim), (shards_of,), jnp.float32, smallest / len(cuts), high / len(cuts)))
        level = level * jnp.repeat(draws, extent[dim] // shards_of).reshape([-1 if axis == dim else 1 for axis in range(len(extent))])
    return level


def scatter_about(own_key, dims, scale, limit, kind=jnp.bfloat16):
    return jnp.clip(scale * jax.random.normal(own_key, dims, jnp.float32), -limit, limit).astype(kind)


def setup_inputs(seed: int = 0) -> dict:
    streams_of = jax.random.split(jax.random.key(seed), 10)
    return {
        "mean_mix": jnp.clip(0.05 + 0.9 * jax.random.uniform(streams_of[0], (NLES,), jnp.float32) ** block_levels(streams_of[0], (NLES,), ((0, 32),), -0.2, 0.2), 0.05, 0.95),
        "segregation": draw_segregation(jax.random.fold_in(streams_of[9], 71), 0),
        "dissipation": jnp.clip(jnp.exp(math.log(0.4) - 2.3025851 * jax.random.uniform(streams_of[2], (NLES,), jnp.float32) ** block_levels(streams_of[2], (NLES,), ((0, 32),), -0.2, 0.2)), 0.04, 0.4),
        "les_map": with_ends(jax.random.randint(streams_of[3], (NLES,), 0, CMC_DEV), jax.random.fold_in(streams_of[3], 1), 0, CMC_DEV - 1).astype(jnp.int32),
        "cond_state": draw_cond_state(jax.random.fold_in(streams_of[9], 71), 0),
        "slot_cell": draw_slot_cell(jax.random.fold_in(streams_of[9], 71), 0),
        "adjacency": with_ends(jax.random.randint(streams_of[6], (4, NCMC), 0, CMC_DEV + 4 * RIM), jax.random.fold_in(streams_of[6], 1), 0, (CMC_DEV + 4 * RIM) - 1).astype(jnp.int32),
        "substeps": draw_substeps(jax.random.fold_in(streams_of[9], 71), 0),
        "coupling": scatter_about(streams_of[8], (K, K), K ** -0.5, 2.0, jnp.float32),
    }


tau_face = 0.12
floor_mass = 0.25


def beta_weights(mean_mix, segregation, bins_count):
    centre = (jnp.arange(bins_count, dtype=jnp.float32) + 0.5) / bins_count
    shape_sum = 1.0 / segregation - 1.0
    shape_low = mean_mix * shape_sum
    shape_high = (1.0 - mean_mix) * shape_sum
    log_weight = (shape_low[None, :] - 1.0) * jnp.log(centre)[:, None] + (shape_high[None, :] - 1.0) * jnp.log(1.0 - centre)[:, None]
    density = jnp.exp(log_weight)
    return density / jnp.sum(density, axis=0, keepdims=True)


def chemistry(start_state, cond_ratio, step_count, coupling):
    step_size = 1.0 / jnp.maximum(step_count, 1.0)

    def advance(substep, cond_now):
        below_bin = jnp.concatenate([cond_now[:, :1], cond_now[:, :-1]], axis=1)
        above_bin = jnp.concatenate([cond_now[:, 1:], cond_now[:, -1:]], axis=1)
        spread = cond_ratio[None] * (above_bin - 2.0 * cond_now + below_bin)
        source = jnp.tanh(jnp.einsum('jk,kbs->jbs', coupling, cond_now, precision=lax.Precision.HIGHEST))
        advanced = cond_now + step_size[None, None] * (spread + source)
        active = substep.astype(jnp.float32) < step_count
        return jnp.where(active[None, None], advanced, cond_now)

    return lax.fori_loop(0, SUBMAX, advance, start_state)


def reference(mean_mix, segregation, dissipation, les_map, cond_state, slot_cell, adjacency, substeps, coupling):
    n_scalar, n_bins, total_cells = cond_state.shape
    tiles = N_GX * N_YZ
    geo_state = jnp.zeros_like(cond_state).at[:, :, slot_cell].set(cond_state)
    geo_steps = jnp.zeros((total_cells,), jnp.float32).at[slot_cell].set(substeps.astype(jnp.float32))
    weights = beta_weights(mean_mix, segregation, n_bins)
    les_count = mean_mix.shape[0]
    tile_of = jnp.arange(les_count, dtype=jnp.int32) // LES_DEV
    cell_id = (tile_of * CMC_DEV + les_map).astype(jnp.int32)
    moments = jnp.concatenate([weights, dissipation[None, :] * weights], axis=0)
    cell_totals = jax.ops.segment_sum(moments.T, cell_id, num_segments=total_cells).T
    cond_ratio = cell_totals[n_bins:] / jnp.maximum(cell_totals[:n_bins], floor_mass)
    cube = geo_state.reshape(n_scalar, n_bins, N_GX, N_YZ, CMC_DEV)
    rim_state = cube[..., :RIM]
    padded = jnp.pad(rim_state, ((0, 0), (0, 0), (1, 1), (1, 1), (0, 0)))
    extended = jnp.concatenate([cube, padded[:, :, :-2, 1:-1], padded[:, :, 2:, 1:-1], padded[:, :, 1:-1, :-2], padded[:, :, 1:-1, 2:]], axis=-1)
    face_map = adjacency.reshape(4, N_GX, N_YZ, CMC_DEV)
    neighbour_sum = jnp.zeros_like(cube)
    for face in range(4):
        face_index = jnp.broadcast_to(face_map[face][None, None], cube.shape)
        neighbour_sum = neighbour_sum + jnp.take_along_axis(extended, face_index, axis=-1)
    moved_cube = cube + tau_face * (neighbour_sum - 4.0 * cube)
    moved_state = moved_cube.reshape(n_scalar, n_bins, total_cells)
    geo_new = chemistry(moved_state, cond_ratio, geo_steps, coupling)
    cond_new = geo_new[:, :, slot_cell]
    tile_weight_all = weights.reshape(n_bins, tiles, LES_DEV).transpose(1, 0, 2)
    tile_map_all = les_map.reshape(tiles, LES_DEV)
    tile_state_all = geo_new.reshape(n_scalar, n_bins, tiles, CMC_DEV).transpose(2, 0, 1, 3)

    def tile_species(packed):
        tile_weight, tile_map, tile_state = packed
        return jnp.sum(tile_weight[None] * jnp.take(tile_state, tile_map, axis=2), axis=1)

    per_tile = lax.map(tile_species, (tile_weight_all, tile_map_all, tile_state_all))
    species = per_tile.transpose(1, 0, 2).reshape(n_scalar, les_count)
    return species, cond_new
```

```python
import functools

import jax
import jax.numpy as jnp
from jax import lax
from jax.experimental import pallas as pl
from jax.experimental.pallas import tpu as pltpu
from jax.sharding import PartitionSpec as P

tau_face = 0.12
floor_mass = 0.25
submax = 8
f32, bf16 = jnp.float32, jnp.bfloat16
NN = (((1,), (0,)), ((), ()))
NT = (((1,), (1,)), ((), ()))
TN = (((0,), (0,)), ((), ()))


def split(x):
    high = x.astype(bf16)
    low = (x - high.astype(f32)).astype(bf16)
    return high, low


def mm(a, b, dims):
    return lax.dot_general(a, b, dims, preferred_element_type=f32)


def iota(shape, dim):
    return lax.broadcasted_iota(jnp.int32, shape, dim)


def onehot(mask):
    return jnp.where(mask, 1.0, 0.0).astype(bf16)


def kernel(
    n_gx, n_yz, cap, chunk,
    mean_ref, seg_ref, diss_ref, map_ref, state_ref, slot_ref, adj_ref, steps_ref, coup_ref,
    species_ref, cond_ref,
    send, recv, reply, back, info_out, info_in, info_rows, halo_out, halo_in,
    weights, ratio, pack, unpack, q0, q1, new_high, new_low, step_row,
    s_send, s_recv, i_send, i_recv, b_send, b_recv, h_send, h_recv,
):
    n_scalar, n_bins, n_cells = state_ref.shape
    rows = n_scalar * n_bins
    n_les = mean_ref.shape[1]
    n = n_gx * n_yz
    slots = send.shape[0]
    capp = slots // n
    rim = halo_out.shape[0]
    gx, yz = lax.axis_index("gx"), lax.axis_index("yz")
    me = gx * n_yz + yz

    def coords(r):
        t = lax.rem(me + r, n)
        return t, (t // n_yz, lax.rem(t, n_yz))

    def block(ref, t):
        return ref.at[pl.ds(pl.multiple_of(t * capp, 8), capp)]

    def info_copy(r):
        t, dev = coords(r)
        return pltpu.make_async_remote_copy(
            info_out.at[t], info_in.at[me], i_send.at[r], i_recv.at[r],
            device_id=dev, device_id_type=pl.DeviceIdType.MESH)

    def state_copy(r):
        t, dev = coords(r)
        return pltpu.make_async_remote_copy(
            block(send, t), block(recv, me), s_send.at[r], s_recv.at[r],
            device_id=dev, device_id_type=pl.DeviceIdType.MESH)

    def back_copy(r):
        t, dev = coords(r)
        return pltpu.make_async_remote_copy(
            block(reply, t), block(back, me), b_send.at[r], b_recv.at[r],
            device_id=dev, device_id_type=pl.DeviceIdType.MESH)

    def each(body):
        def run(r, carry):
            body(r)
            return carry
        lax.fori_loop(1, n, run, 0)

    halo_in[...] = jnp.zeros_like(halo_in)
    barrier = pltpu.get_barrier_semaphore()

    def greet(r):
        _, dev = coords(r)
        pl.semaphore_signal(barrier, inc=1, device_id=dev, device_id_type=pl.DeviceIdType.MESH)

    each(greet)

    slot = slot_ref[...]
    home = slot // n_cells
    local = slot - home * n_cells
    marks = iota((n, n_cells), 0) == home
    before = onehot(iota((n_cells, n_cells), 0) < iota((n_cells, n_cells), 1))
    earlier = mm(onehot(marks), before, NN)
    marks_f = jnp.where(marks, 1.0, 0.0)
    position = jnp.sum(earlier * marks_f, axis=0, keepdims=True).astype(jnp.int32)
    send_pos = home * capp + position
    pack[...] = onehot(iota((slots, n_cells), 0) == send_pos)

    lane = iota((128, n_cells), 0)
    at_low = onehot(lane == position)
    at_high = onehot(lane - 64 == position)
    index_part = (marks_f * (local + 1).astype(f32)).astype(bf16)
    steps_part = (marks_f * steps_ref[...].astype(f32)).astype(bf16)
    info = mm(index_part, at_low, NT) + mm(steps_part, at_high, NT)
    for d in range(n):
        info_out[d] = info[d:d + 1, :]

    high, low = split(state_ref[...].reshape(rows, n_cells))
    send[...] = mm(pack[...], high, NT) + mm(pack[...], low, NT)

    pl.semaphore_wait(barrier, n - 1)
    each(lambda r: info_copy(r).start())
    each(lambda r: state_copy(r).start())
    info_in[pl.ds(me, 1)] = info_out[pl.ds(me, 1)]
    mine = pl.ds(pl.multiple_of(me * capp, 8), capp)
    recv[mine, :] = send[mine, :]

    centre = (iota((n_bins, 128), 0).astype(f32) + 0.5) / n_bins
    log_low = jnp.log(centre)[:, :1]
    log_high = jnp.log(1.0 - centre)[:, :1]
    ratio[...] = jnp.zeros_like(ratio)

    def les_part(i, carry):
        part = pl.ds(pl.multiple_of(i * chunk, chunk), chunk)
        mean = mean_ref[:, part]
        shape_sum = 1.0 / seg_ref[:, part] - 1.0
        shape_low = mean * shape_sum
        shape_high = (1.0 - mean) * shape_sum
        density = jnp.exp((shape_low - 1.0) * log_low + (shape_high - 1.0) * log_high)
        w = density / jnp.sum(density, axis=0, keepdims=True)
        weights[:, part] = w
        moments = jnp.concatenate([w, diss_ref[:, part] * w], axis=0)
        m_high, m_low = split(moments)
        member = onehot(iota((n_cells, chunk), 0) == map_ref[:, part])
        ratio[...] += mm(m_high, member, NT) + mm(m_low, member, NT)
        return carry

    lax.fori_loop(0, n_les // chunk, les_part, 0)
    ratio[:n_bins, :] = ratio[n_bins:, :] / jnp.maximum(ratio[:n_bins, :], floor_mass)

    each(lambda r: info_copy(r).wait_recv())
    for d in range(n):
        info_rows[d:d + 1, :] = info_in[d]
    table = info_rows[...].astype(bf16)
    spread = onehot(iota((slots, n), 0) // capp == iota((slots, n), 1))
    wide = mm(spread, table, NN)
    slot_in = lax.rem(iota((slots, 128), 0), capp)
    lanes = iota((slots, 128), 1)
    index_col = jnp.sum(jnp.where(lanes == slot_in, wide, 0.0), axis=1, keepdims=True)
    steps_col = jnp.sum(jnp.where(lanes == slot_in + 64, wide, 0.0), axis=1, keepdims=True)
    placed = index_col.astype(jnp.int32) == iota((slots, n_cells), 1) + 1
    unpack[...] = onehot(placed)
    step_row[...] = jnp.sum(jnp.where(placed, steps_col, 0.0), axis=0, keepdims=True)
    counts = jnp.zeros((n_cells + 4 * rim, n_cells), f32)
    entry = iota((n_cells + 4 * rim, n_cells), 0)
    for face in range(4):
        counts = counts + jnp.where(adj_ref[face:face + 1, :] == entry, 1.0, 0.0)
    counts = counts.astype(bf16)

    each(lambda r: state_copy(r).wait_recv())
    g_high, g_low = split(recv[...])
    rim_pick = unpack[:, :128]
    halo_out[...] = (mm(rim_pick, g_high, TN) + mm(rim_pick, g_low, TN))[:rim]

    beside = (
        (gx < n_gx - 1, (gx + 1, yz), 0, gx > 0),
        (gx > 0, (gx - 1, yz), 1, gx < n_gx - 1),
        (yz < n_yz - 1, (gx, yz + 1), 2, yz > 0),
        (yz > 0, (gx, yz - 1), 3, yz < n_yz - 1),
    )

    def halo_copy(dev, place):
        return pltpu.make_async_remote_copy(
            halo_out, halo_in.at[pl.ds(place * rim, rim)], h_send.at[place], h_recv.at[place],
            device_id=dev, device_id_type=pl.DeviceIdType.MESH)

    for there, dev, place, _ in beside:
        @pl.when(there)
        def _start():
            halo_copy(dev, place).start()

    home_state = mm(g_high, unpack[...], TN) + mm(g_low, unpack[...], TN)
    o_high, o_low = split(home_state)
    own_counts = counts[:n_cells]
    moved = home_state * (1.0 - 4.0 * tau_face) + tau_face * (
        mm(o_high, own_counts, NN) + mm(o_low, own_counts, NN))
    for _, dev, place, from_there in beside:
        @pl.when(from_there)
        def _wait():
            halo_copy(dev, place).wait_recv()
    r_high, r_low = split(halo_in[...])
    far_counts = counts[n_cells:]
    moved = moved + tau_face * (mm(r_high, far_counts, TN) + mm(r_low, far_counts, TN))
    q0[...] = moved.reshape(n_scalar, n_bins, n_cells)

    count = step_row[...]
    size = 1.0 / jnp.maximum(count, 1.0)
    bins_at = iota((n_bins, n_cells), 0)
    first, last = bins_at == 0, bins_at == n_bins - 1

    def substep(src, dst, s):
        h = jnp.where(s.astype(f32) < count, size, 0.0)
        rate = ratio[:n_bins, :] * h
        for j in range(n_scalar):
            mixed = coup_ref[j, 0] * src[0]
            for k in range(1, n_scalar):
                mixed = mixed + coup_ref[j, k] * src[k]
            q = src[j]
            below = jnp.where(first, q, pltpu.roll(q, 1, 0))
            above = jnp.where(last, q, pltpu.roll(q, n_bins - 1, 0))
            dst[j] = q + rate * (above - 2.0 * q + below) + h * jnp.tanh(mixed)

    def pair(i, carry):
        substep(q0, q1, 2 * i)
        substep(q1, q0, 2 * i + 1)
        return carry

    lax.fori_loop(0, submax // 2, pair, 0)

    n_high, n_low = split(q0[...].reshape(rows, n_cells))
    new_high[...] = n_high
    new_low[...] = n_low
    reply[...] = mm(unpack[...], n_high, NT) + mm(unpack[...], n_low, NT)
    each(lambda r: back_copy(r).start())
    back[mine, :] = reply[mine, :]

    def species_part(i, carry):
        part = pl.ds(pl.multiple_of(i * chunk, chunk), chunk)
        member = onehot(iota((n_cells, chunk), 0) == map_ref[:, part])
        w = weights[:, part]
        picked = mm(new_high[...], member, NN) + mm(new_low[...], member, NN)
        for k in range(n_scalar):
            species_ref[k:k + 1, part] = jnp.sum(
                picked[k * n_bins:(k + 1) * n_bins] * w, axis=0, keepdims=True)
        return carry

    lax.fori_loop(0, n_les // chunk, species_part, 0)

    each(lambda r: back_copy(r).wait_recv())
    b_high, b_low = split(back[...])
    cond_ref[...] = (mm(b_high, pack[...], TN) + mm(b_low, pack[...], TN)).reshape(
        n_scalar, n_bins, n_cells)

    def drain(r):
        info_copy(r).wait_send()
        state_copy(r).wait_send()
        back_copy(r).wait_send()

    each(drain)
    for there, dev, place, _ in beside:
        @pl.when(there)
        def _drain():
            halo_copy(dev, place).wait_send()


def shards(n_gx, n_yz, mean_mix, segregation, dissipation, les_map, cond_state, slot_cell,
           adjacency, substeps, coupling):
    n_scalar, n_bins, n_cells = cond_state.shape
    n_les = mean_mix.shape[0]
    n = n_gx * n_yz
    rows = n_scalar * n_bins
    cap = 2 * n_cells // n
    capp = -(-cap // 8) * 8
    slots = n * capp
    rim = n_cells // 8
    chunk = min(512, n_les)
    vmem = pl.BlockSpec(memory_space=pltpu.VMEM)
    dma = pltpu.SemaphoreType.DMA
    return pl.pallas_call(
        functools.partial(kernel, n_gx, n_yz, cap, chunk),
        out_shape=(
            jax.ShapeDtypeStruct((n_scalar, n_les), f32),
            jax.ShapeDtypeStruct((n_scalar, n_bins, n_cells), f32),
        ),
        in_specs=[vmem] * 8 + [pl.BlockSpec(memory_space=pltpu.SMEM)],
        out_specs=(vmem, vmem),
        scratch_shapes=[
            pltpu.VMEM((slots, rows), f32),
            pltpu.VMEM((slots, rows), f32),
            pltpu.VMEM((slots, rows), f32),
            pltpu.VMEM((slots, rows), f32),
            pltpu.VMEM((n, 1, 128), f32),
            pltpu.VMEM((n, 1, 128), f32),
            pltpu.VMEM((n, 128), f32),
            pltpu.VMEM((rim, rows), f32),
            pltpu.VMEM((4 * rim, rows), f32),
            pltpu.VMEM((n_bins, n_les), f32),
            pltpu.VMEM((2 * n_bins, n_cells), f32),
            pltpu.VMEM((slots, n_cells), bf16),
            pltpu.VMEM((slots, n_cells), bf16),
            pltpu.VMEM((n_scalar, n_bins, n_cells), f32),
            pltpu.VMEM((n_scalar, n_bins, n_cells), f32),
            pltpu.VMEM((rows, n_cells), bf16),
            pltpu.VMEM((rows, n_cells), bf16),
            pltpu.VMEM((1, n_cells), f32),
            dma((n,)), dma((n,)), dma((n,)), dma((n,)), dma((n,)), dma((n,)), dma((4,)), dma((4,)),
        ],
        compiler_params=pltpu.CompilerParams(
            collective_id=0, has_side_effects=True, vmem_limit_bytes=48 * 1024 * 1024),
        cost_estimate=pl.CostEstimate(
            flops=8 * rows * n_les * n_cells, bytes_accessed=4 * rows * n_cells,
            transcendentals=n_bins * n_les),
    )(
        mean_mix.reshape(1, n_les), segregation.reshape(1, n_les), dissipation.reshape(1, n_les),
        les_map.reshape(1, n_les), cond_state, slot_cell.reshape(1, n_cells), adjacency,
        substeps.reshape(1, n_cells), coupling,
    )


def solution(mesh):
    both = P(("gx", "yz"))
    placed = (both, both, both, both, P(None, None, ("gx", "yz")), both,
              P(None, ("gx", "yz")), both, P())
    return jax.shard_map(
        functools.partial(shards, mesh.shape["gx"], mesh.shape["yz"]),
        mesh=mesh,
        in_specs=placed,
        out_specs=(P(None, ("gx", "yz")), P(None, None, ("gx", "yz"))),
        check_vma=False,
    )
```

```python
import functools

import jax
import jax.numpy as jnp
from jax import lax
from jax.experimental import pallas as pl
from jax.experimental.pallas import tpu as pltpu
from jax.sharding import PartitionSpec as P

tau_face = 0.12
floor_mass = 0.25
submax = 8
f32, bf16 = jnp.float32, jnp.bfloat16
NN = (((1,), (0,)), ((), ()))
NT = (((1,), (1,)), ((), ()))
TN = (((0,), (0,)), ((), ()))


def split(x):
    high = x.astype(bf16)
    low = (x - high.astype(f32)).astype(bf16)
    return high, low


def mm(a, b, dims):
    return lax.dot_general(a, b, dims, preferred_element_type=f32)


def iota(shape, dim):
    return lax.broadcasted_iota(jnp.int32, shape, dim)


def onehot(mask):
    return jnp.where(mask, 1.0, 0.0).astype(bf16)


def kernel(
    n_gx, n_yz, cap, chunk,
    mean_hbm, seg_hbm, diss_hbm, map_hbm, state_hbm, slot_hbm, adj_hbm, steps_hbm, coup_hbm,
    species_ref, cond_ref,
    mean_ref, seg_ref, diss_ref, map_ref, state_ref, slot_ref, adj_ref, steps_ref, coup_ref,
    send, recv, reply, back, info_out, info_in, info_rows, halo_out, halo_in,
    weights, ratio, pack, unpack, q0, q1, new_high, new_low, step_row, rim_sum,
    a_sem,    s_send, s_recv, i_send, i_recv, b_send, b_recv, h_send, h_recv,
):
    n_scalar, n_bins, n_cells = state_ref.shape
    rows = n_scalar * n_bins
    n_les = mean_ref.shape[1]
    n = n_gx * n_yz
    slots = send.shape[0]
    capp = slots // n
    rim = halo_out.shape[0]
    gx, yz = lax.axis_index("gx"), lax.axis_index("yz")
    mesh_id = pl.DeviceIdType.MESH
    half = n_gx // 2
    groups = 4
    per = n // groups
    width = slots // groups

    def steps_of(b):
        i = b // n_yz
        odd = lax.rem(i, 2)
        dg = lax.rem(half + (1 - 2 * odd) * ((i + 1) // 2) + n_gx, n_gx)
        return dg, n_yz - 1 - lax.rem(b, n_yz)

    def ahead(b):
        dg, dy = steps_of(b)
        return lax.rem(gx + dg, n_gx), lax.rem(yz + dy, n_yz)

    def behind(b):
        dg, dy = steps_of(b)
        return lax.rem(gx - dg + n_gx, n_gx), lax.rem(yz - dy + n_yz, n_yz)

    def block(ref, b):
        return ref.at[pl.ds(pl.multiple_of(b * capp, 8), capp)]

    def info_copy(b):
        return pltpu.make_async_remote_copy(
            info_out.at[b], info_in.at[b], i_send.at[b], i_recv.at[b],
            device_id=ahead(b), device_id_type=mesh_id)

    def state_copy(b):
        return pltpu.make_async_remote_copy(
            block(send, b), block(recv, b), s_send.at[b], s_recv.at[b],
            device_id=ahead(b), device_id_type=mesh_id)

    def back_copy(b):
        return pltpu.make_async_remote_copy(
            block(reply, b), block(back, b), b_send.at[b], b_recv.at[b],
            device_id=behind(b), device_id_type=mesh_id)

    def each(body, low=0, high=n - 1):
        def run(b, carry):
            body(b)
            return carry
        lax.fori_loop(low, high, run, 0)

    def each_of(group, body):
        each(body, group * per, min((group + 1) * per, n - 1))

    def rows_of(group):
        return pl.ds(group * width, width)

    fetches = [
        pltpu.make_async_copy(src, dst, a_sem.at[i])
        for i, (src, dst) in enumerate((
            (slot_hbm, slot_ref), (steps_hbm, steps_ref), (state_hbm, state_ref),
            (mean_hbm, mean_ref), (seg_hbm, seg_ref), (diss_hbm, diss_ref),
            (map_hbm, map_ref), (adj_hbm, adj_ref), (coup_hbm, coup_ref)))
    ]
    for fetch in fetches:
        fetch.start()

    halo_in[...] = jnp.zeros_like(halo_in)
    barrier = pltpu.get_barrier_semaphore()

    def greet(b):
        pl.semaphore_signal(barrier, inc=1, device_id=ahead(b), device_id_type=mesh_id)

    each(greet)

    fetches[0].wait()
    fetches[1].wait()
    slot = slot_ref[...]
    tile = slot // n_cells
    local = slot - tile * n_cells
    tile_g = tile // n_yz
    from_half = lax.rem(tile_g - gx + n_gx, n_gx) - half
    step_i = jnp.where(from_half >= 0, 2 * from_half, -2 * from_half - 1)
    home = step_i * n_yz + n_yz - 1 - lax.rem(tile - tile_g * n_yz - yz + n_yz, n_yz)
    marks = iota((n, n_cells), 0) == home
    before = onehot(iota((n_cells, n_cells), 0) < iota((n_cells, n_cells), 1))
    earlier = mm(onehot(marks), before, NN)
    marks_f = jnp.where(marks, 1.0, 0.0)
    position = jnp.sum(earlier * marks_f, axis=0, keepdims=True).astype(jnp.int32)
    send_pos = home * capp + position
    pack[...] = onehot(iota((slots, n_cells), 0) == send_pos)

    lane = iota((128, n_cells), 0)
    at_low = onehot(lane == position)
    at_high = onehot(lane - 64 == position)
    index_part = (marks_f * (local + 1).astype(f32)).astype(bf16)
    steps_part = (marks_f * steps_ref[...].astype(f32)).astype(bf16)
    info = mm(index_part, at_low, NT) + mm(steps_part, at_high, NT)
    for d in range(n):
        info_out[d] = info[d:d + 1, :]

    fetches[2].wait()
    high, low = split(state_ref[...].reshape(rows, n_cells))
    send[rows_of(0), :] = mm(pack[rows_of(0), :], high, NT) + mm(pack[rows_of(0), :], low, NT)
    pl.semaphore_wait(barrier, n - 1)
    each(lambda b: info_copy(b).start())
    each_of(0, lambda b: state_copy(b).start())
    for g in range(1, groups):
        part = rows_of(g)
        send[part, :] = mm(pack[part, :], high, NT) + mm(pack[part, :], low, NT)
        each_of(g, lambda b: state_copy(b).start())
    info_in[n - 1] = info_out[n - 1]
    mine = pl.ds(slots - capp, capp)
    recv[mine, :] = send[mine, :]
    for fetch in fetches[3:]:
        fetch.wait()

    centre = (iota((n_bins, 128), 0).astype(f32) + 0.5) / n_bins
    log_low = jnp.log(centre)[:, :1]
    log_high = jnp.log(1.0 - centre)[:, :1]
    ratio[...] = jnp.zeros_like(ratio)

    def les_part(i, carry):
        part = pl.ds(pl.multiple_of(i * chunk, chunk), chunk)
        mean = mean_ref[:, part]
        shape_sum = 1.0 / seg_ref[:, part] - 1.0
        shape_low = mean * shape_sum
        shape_high = (1.0 - mean) * shape_sum
        density = jnp.exp((shape_low - 1.0) * log_low + (shape_high - 1.0) * log_high)
        w = density / jnp.sum(density, axis=0, keepdims=True)
        weights[:, part] = w
        moments = jnp.concatenate([w, diss_ref[:, part] * w], axis=0)
        m_high, m_low = split(moments)
        member = onehot(iota((n_cells, chunk), 0) == map_ref[:, part])
        ratio[...] += mm(m_high, member, NT) + mm(m_low, member, NT)
        return carry

    lax.fori_loop(0, n_les // chunk, les_part, 0)
    ratio[:n_bins, :] = ratio[n_bins:, :] / jnp.maximum(ratio[:n_bins, :], floor_mass)

    each(lambda b: info_copy(b).wait_recv())
    for d in range(n):
        info_rows[d:d + 1, :] = info_in[d]
    table = info_rows[...].astype(bf16)
    spread = onehot(iota((slots, n), 0) // capp == iota((slots, n), 1))
    wide = mm(spread, table, NN)
    slot_in = lax.rem(iota((slots, 128), 0), capp)
    lanes = iota((slots, 128), 1)
    index_col = jnp.sum(jnp.where(lanes == slot_in, wide, 0.0), axis=1, keepdims=True)
    steps_col = jnp.sum(jnp.where(lanes == slot_in + 64, wide, 0.0), axis=1, keepdims=True)
    placed = index_col.astype(jnp.int32) == iota((slots, n_cells), 1) + 1
    unpack[...] = onehot(placed)
    step_row[...] = jnp.sum(jnp.where(placed, steps_col, 0.0), axis=0, keepdims=True)
    counts = jnp.zeros((n_cells + 4 * rim, n_cells), f32)
    entry = iota((n_cells + 4 * rim, n_cells), 0)
    for face in range(4):
        counts = counts + jnp.where(adj_ref[face:face + 1, :] == entry, 1.0, 0.0)
    counts = counts.astype(bf16)

    for g in range(groups):
        part = rows_of(g)
        each_of(g, lambda b: state_copy(b).wait_recv())
        g_high, g_low = split(recv[part, :])
        into = unpack[part, :]
        more = mm(g_high, into, TN) + mm(g_low, into, TN)
        rim_more = mm(into[:, :128], g_high, TN) + mm(into[:, :128], g_low, TN)
        more = more.reshape(n_scalar, n_bins, n_cells)
        if g == 0:
            q1[...] = more
            rim_sum[...] = rim_more
        elif g < groups - 1:
            q1[...] += more
            rim_sum[...] += rim_more
        else:
            halo_out[...] = (rim_sum[...] + rim_more)[:rim]
            q1[...] += more

    beside = (
        (gx < n_gx - 1, (gx + 1, yz), 0, gx > 0),
        (gx > 0, (gx - 1, yz), 1, gx < n_gx - 1),
        (yz < n_yz - 1, (gx, yz + 1), 2, yz > 0),
        (yz > 0, (gx, yz - 1), 3, yz < n_yz - 1),
    )

    def halo_copy(dev, place):
        return pltpu.make_async_remote_copy(
            halo_out, halo_in.at[pl.ds(place * rim, rim)], h_send.at[place], h_recv.at[place],
            device_id=dev, device_id_type=mesh_id)

    for there, dev, place, _ in beside:
        @pl.when(there)
        def _start():
            halo_copy(dev, place).start()

    home_state = q1[...].reshape(rows, n_cells)
    o_high, o_low = split(home_state)
    own_counts = counts[:n_cells]
    moved = home_state * (1.0 - 4.0 * tau_face) + tau_face * (
        mm(o_high, own_counts, NN) + mm(o_low, own_counts, NN))
    for _, dev, place, from_there in beside:
        @pl.when(from_there)
        def _wait():
            halo_copy(dev, place).wait_recv()
    r_high, r_low = split(halo_in[...])
    far_counts = counts[n_cells:]
    moved = moved + tau_face * (mm(r_high, far_counts, TN) + mm(r_low, far_counts, TN))
    q0[...] = moved.reshape(n_scalar, n_bins, n_cells)

    count = step_row[...]
    size = 1.0 / jnp.maximum(count, 1.0)
    bins_at = iota((n_bins, n_cells), 0)
    first, last = bins_at == 0, bins_at == n_bins - 1

    def substep(src, dst, s):
        h = jnp.where(s.astype(f32) < count, size, 0.0)
        rate = ratio[:n_bins, :] * h
        for j in range(n_scalar):
            mixed = coup_ref[j, 0] * src[0]
            for k in range(1, n_scalar):
                mixed = mixed + coup_ref[j, k] * src[k]
            q = src[j]
            below = jnp.where(first, q, pltpu.roll(q, 1, 0))
            above = jnp.where(last, q, pltpu.roll(q, n_bins - 1, 0))
            dst[j] = q + rate * (above - 2.0 * q + below) + h * jnp.tanh(mixed)

    def pair(i, carry):
        substep(q0, q1, 2 * i)
        substep(q1, q0, 2 * i + 1)
        return carry

    lax.fori_loop(0, submax // 2, pair, 0)

    n_high, n_low = split(q0[...].reshape(rows, n_cells))
    new_high[...] = n_high
    new_low[...] = n_low
    for g in range(groups):
        part = rows_of(g)
        reply[part, :] = mm(unpack[part, :], n_high, NT) + mm(unpack[part, :], n_low, NT)
        each_of(g, lambda b: back_copy(b).start())
    back[mine, :] = reply[mine, :]

    def species_part(i, carry):
        part = pl.ds(pl.multiple_of(i * chunk, chunk), chunk)
        member = onehot(iota((n_cells, chunk), 0) == map_ref[:, part])
        w = weights[:, part]
        picked = mm(new_high[...], member, NN) + mm(new_low[...], member, NN)
        for k in range(n_scalar):
            species_ref[k:k + 1, part] = jnp.sum(
                picked[k * n_bins:(k + 1) * n_bins] * w, axis=0, keepdims=True)
        return carry

    lax.fori_loop(0, n_les // chunk, species_part, 0)

    for g in range(groups):
        part = rows_of(g)
        each_of(g, lambda b: back_copy(b).wait_recv())
        b_high, b_low = split(back[part, :])
        more = (mm(b_high, pack[part, :], TN) + mm(b_low, pack[part, :], TN)).reshape(
            n_scalar, n_bins, n_cells)
        if g == 0:
            cond_ref[...] = more
        else:
            cond_ref[...] += more

    def drain(r):
        info_copy(r).wait_send()
        state_copy(r).wait_send()
        back_copy(r).wait_send()

    each(drain)
    for there, dev, place, _ in beside:
        @pl.when(there)
        def _drain():
            halo_copy(dev, place).wait_send()


def shards(n_gx, n_yz, mean_mix, segregation, dissipation, les_map, cond_state, slot_cell,
           adjacency, substeps, coupling):
    n_scalar, n_bins, n_cells = cond_state.shape
    n_les = mean_mix.shape[0]
    n = n_gx * n_yz
    rows = n_scalar * n_bins
    cap = 2 * n_cells // n
    capp = -(-cap // 8) * 8
    slots = n * capp
    rim = n_cells // 8
    chunk = min(512, n_les)
    vmem = pl.BlockSpec(memory_space=pltpu.VMEM)
    dma = pltpu.SemaphoreType.DMA
    return pl.pallas_call(
        functools.partial(kernel, n_gx, n_yz, cap, chunk),
        out_shape=(
            jax.ShapeDtypeStruct((n_scalar, n_les), f32),
            jax.ShapeDtypeStruct((n_scalar, n_bins, n_cells), f32),
        ),
        in_specs=[pl.BlockSpec(memory_space=pltpu.HBM)] * 9,
        out_specs=(vmem, vmem),
        scratch_shapes=[
            pltpu.VMEM((1, n_les), f32),
            pltpu.VMEM((1, n_les), f32),
            pltpu.VMEM((1, n_les), f32),
            pltpu.VMEM((1, n_les), jnp.int32),
            pltpu.VMEM((n_scalar, n_bins, n_cells), f32),
            pltpu.VMEM((1, n_cells), jnp.int32),
            pltpu.VMEM((4, n_cells), jnp.int32),
            pltpu.VMEM((1, n_cells), jnp.int32),
            pltpu.SMEM(coupling.shape, f32),
            pltpu.VMEM((slots, rows), f32),
            pltpu.VMEM((slots, rows), f32),
            pltpu.VMEM((slots, rows), f32),
            pltpu.VMEM((slots, rows), f32),
            pltpu.VMEM((n, 1, 128), f32),
            pltpu.VMEM((n, 1, 128), f32),
            pltpu.VMEM((n, 128), f32),
            pltpu.VMEM((rim, rows), f32),
            pltpu.VMEM((4 * rim, rows), f32),
            pltpu.VMEM((n_bins, n_les), f32),
            pltpu.VMEM((2 * n_bins, n_cells), f32),
            pltpu.VMEM((slots, n_cells), bf16),
            pltpu.VMEM((slots, n_cells), bf16),
            pltpu.VMEM((n_scalar, n_bins, n_cells), f32),
            pltpu.VMEM((n_scalar, n_bins, n_cells), f32),
            pltpu.VMEM((rows, n_cells), bf16),
            pltpu.VMEM((rows, n_cells), bf16),
            pltpu.VMEM((1, n_cells), f32),
            pltpu.VMEM((128, rows), f32),
            dma((9,)), dma((n,)), dma((n,)), dma((n,)), dma((n,)), dma((n,)), dma((n,)), dma((4,)), dma((4,)),
        ],
        compiler_params=pltpu.CompilerParams(
            collective_id=0, has_side_effects=True, vmem_limit_bytes=48 * 1024 * 1024),
        cost_estimate=pl.CostEstimate(
            flops=8 * rows * n_les * n_cells, bytes_accessed=4 * rows * n_cells,
            transcendentals=n_bins * n_les),
    )(
        mean_mix.reshape(1, n_les), segregation.reshape(1, n_les), dissipation.reshape(1, n_les),
        les_map.reshape(1, n_les), cond_state, slot_cell.reshape(1, n_cells), adjacency,
        substeps.reshape(1, n_cells), coupling,
    )


def solution(mesh):
    both = P(("gx", "yz"))
    placed = (both, both, both, both, P(None, None, ("gx", "yz")), both,
              P(None, ("gx", "yz")), both, P())
    return jax.shard_map(
        functools.partial(shards, mesh.shape["gx"], mesh.shape["yz"]),
        mesh=mesh,
        in_specs=placed,
        out_specs=(P(None, ("gx", "yz")), P(None, None, ("gx", "yz"))),
        check_vma=False,
    )
```

```python
import functools

import jax
import jax.numpy as jnp
from jax import lax
from jax.experimental import pallas as pl
from jax.experimental.pallas import tpu as pltpu
from jax.sharding import PartitionSpec as P

tau_face = 0.12
floor_mass = 0.25
submax = 8
f32, bf16 = jnp.float32, jnp.bfloat16
NN = (((1,), (0,)), ((), ()))
NT = (((1,), (1,)), ((), ()))
TN = (((0,), (0,)), ((), ()))


def split(x):
    high = x.astype(bf16)
    low = (x - high.astype(f32)).astype(bf16)
    return high, low


def mm(a, b, dims):
    return lax.dot_general(a, b, dims, preferred_element_type=f32)


def iota(shape, dim):
    return lax.broadcasted_iota(jnp.int32, shape, dim)


def onehot(mask):
    return jnp.where(mask, 1.0, 0.0).astype(bf16)


def kernel(
    n_gx, n_yz, cap, chunk,
    mean_hbm, seg_hbm, diss_hbm, map_hbm, state_hbm, slot_hbm, adj_hbm, steps_hbm, coup_hbm,
    species_ref, cond_ref,
    mean_ref, seg_ref, diss_ref, map_ref, state_ref, slot_ref, adj_ref, steps_ref, coup_ref,
    send, recv, reply, back, info_out, info_in, info_rows, halo_out, halo_in,
    weights, ratio, pack, unpack, q0, q1, new_high, new_low, step_row, rim_sum,
    a_sem,    s_send, s_recv, i_send, i_recv, b_send, b_recv, h_send, h_recv,
):
    n_scalar, n_bins, n_cells = state_ref.shape
    rows = n_scalar * n_bins
    n_les = mean_ref.shape[1]
    n = n_gx * n_yz
    slots = send.shape[0]
    capp = slots // n
    rim = halo_out.shape[0]
    gx, yz = lax.axis_index("gx"), lax.axis_index("yz")
    mesh_id = pl.DeviceIdType.MESH
    half = n_gx // 2
    groups = 4
    width = slots // groups

    def wrap(a, size):
        a = jnp.where(a >= size, a - size, a)
        return jnp.where(a < 0, a + size, a)

    def dg_of(i):
        odd = i - 2 * (i // 2)
        return half + (1 - 2 * odd) * ((i + 1) // 2)

    def ahead(b):
        i, j = b
        return wrap(gx + dg_of(i), n_gx), wrap(yz + (n_yz - 1 - j), n_yz)

    def behind(b):
        i, j = b
        return wrap(gx - dg_of(i), n_gx), wrap(yz - (n_yz - 1 - j), n_yz)

    def number(b):
        return b[0] * n_yz + b[1]

    def block(ref, b):
        return ref.at[pl.ds(pl.multiple_of(number(b) * capp, 8), capp)]

    def info_copy(b):
        m = number(b)
        return pltpu.make_async_remote_copy(
            info_out.at[m], info_in.at[m], i_send.at[m], i_recv.at[m],
            device_id=ahead(b), device_id_type=mesh_id)

    def state_copy(b):
        m = number(b)
        return pltpu.make_async_remote_copy(
            block(send, b), block(recv, b), s_send.at[m], s_recv.at[m],
            device_id=ahead(b), device_id_type=mesh_id)

    def back_copy(b):
        m = number(b)
        return pltpu.make_async_remote_copy(
            block(reply, b), block(back, b), b_send.at[m], b_recv.at[m],
            device_id=behind(b), device_id_type=mesh_id)

    def each(body, low=0, high=n_gx):
        def run(i, carry):
            for j in range(n_yz):
                body((i, j))
            return carry
        lax.fori_loop(low, min(high, n_gx - 1), run, 0)
        if high == n_gx:
            for j in range(n_yz - 1):
                body((n_gx - 1, j))

    def each_of(group, body):
        each(body, group * (n_gx // groups), (group + 1) * (n_gx // groups))

    def rows_of(group):
        return pl.ds(group * width, width)

    fetches = [
        pltpu.make_async_copy(src, dst, a_sem.at[i])
        for i, (src, dst) in enumerate((
            (slot_hbm, slot_ref), (steps_hbm, steps_ref), (state_hbm, state_ref),
            (mean_hbm, mean_ref), (seg_hbm, seg_ref), (diss_hbm, diss_ref),
            (map_hbm, map_ref), (adj_hbm, adj_ref), (coup_hbm, coup_ref)))
    ]
    for fetch in fetches:
        fetch.start()

    halo_in[...] = jnp.zeros_like(halo_in)
    barrier = pltpu.get_barrier_semaphore()

    def greet(b):
        pl.semaphore_signal(barrier, inc=1, device_id=ahead(b), device_id_type=mesh_id)

    each(greet)

    fetches[0].wait()
    fetches[1].wait()
    slot = slot_ref[...]
    tile = slot // n_cells
    local = slot - tile * n_cells
    tile_g = tile // n_yz
    from_half = lax.rem(tile_g - gx + n_gx, n_gx) - half
    step_i = jnp.where(from_half >= 0, 2 * from_half, -2 * from_half - 1)
    home = step_i * n_yz + n_yz - 1 - lax.rem(tile - tile_g * n_yz - yz + n_yz, n_yz)
    marks = iota((n, n_cells), 0) == home
    before = onehot(iota((n_cells, n_cells), 0) < iota((n_cells, n_cells), 1))
    earlier = mm(onehot(marks), before, NN)
    marks_f = jnp.where(marks, 1.0, 0.0)
    position = jnp.sum(earlier * marks_f, axis=0, keepdims=True).astype(jnp.int32)
    send_pos = home * capp + position
    pack[...] = onehot(iota((slots, n_cells), 0) == send_pos)

    lane = iota((128, n_cells), 0)
    at_low = onehot(lane == position)
    at_high = onehot(lane - 64 == position)
    index_part = (marks_f * (local + 1).astype(f32)).astype(bf16)
    steps_part = (marks_f * steps_ref[...].astype(f32)).astype(bf16)
    info = mm(index_part, at_low, NT) + mm(steps_part, at_high, NT)
    for d in range(n):
        info_out[d] = info[d:d + 1, :]

    fetches[2].wait()
    high, low = split(state_ref[...].reshape(rows, n_cells))
    send[rows_of(0), :] = mm(pack[rows_of(0), :], high, NT) + mm(pack[rows_of(0), :], low, NT)
    pl.semaphore_wait(barrier, n - 1)
    each(lambda b: info_copy(b).start())
    each_of(0, lambda b: state_copy(b).start())
    for g in range(1, groups):
        part = rows_of(g)
        send[part, :] = mm(pack[part, :], high, NT) + mm(pack[part, :], low, NT)
        each_of(g, lambda b: state_copy(b).start())
    info_in[n - 1] = info_out[n - 1]
    mine = pl.ds(slots - capp, capp)
    recv[mine, :] = send[mine, :]
    for fetch in fetches[3:]:
        fetch.wait()

    centre = (iota((n_bins, 128), 0).astype(f32) + 0.5) / n_bins
    log_low = jnp.log(centre)[:, :1]
    log_high = jnp.log(1.0 - centre)[:, :1]
    ratio[...] = jnp.zeros_like(ratio)

    def les_part(i, carry):
        part = pl.ds(pl.multiple_of(i * chunk, chunk), chunk)
        mean = mean_ref[:, part]
        shape_sum = 1.0 / seg_ref[:, part] - 1.0
        shape_low = mean * shape_sum
        shape_high = (1.0 - mean) * shape_sum
        density = jnp.exp((shape_low - 1.0) * log_low + (shape_high - 1.0) * log_high)
        w = density / jnp.sum(density, axis=0, keepdims=True)
        weights[:, part] = w
        moments = jnp.concatenate([w, diss_ref[:, part] * w], axis=0)
        m_high, m_low = split(moments)
        member = onehot(iota((n_cells, chunk), 0) == map_ref[:, part])
        ratio[...] += mm(m_high, member, NT) + mm(m_low, member, NT)
        return carry

    lax.fori_loop(0, n_les // chunk, les_part, 0)
    ratio[:n_bins, :] = ratio[n_bins:, :] / jnp.maximum(ratio[:n_bins, :], floor_mass)

    each(lambda b: info_copy(b).wait_recv())
    for d in range(n):
        info_rows[d:d + 1, :] = info_in[d]
    table = info_rows[...].astype(bf16)
    spread = onehot(iota((slots, n), 0) // capp == iota((slots, n), 1))
    wide = mm(spread, table, NN)
    slot_in = lax.rem(iota((slots, 128), 0), capp)
    lanes = iota((slots, 128), 1)
    index_col = jnp.sum(jnp.where(lanes == slot_in, wide, 0.0), axis=1, keepdims=True)
    steps_col = jnp.sum(jnp.where(lanes == slot_in + 64, wide, 0.0), axis=1, keepdims=True)
    placed = index_col.astype(jnp.int32) == iota((slots, n_cells), 1) + 1
    unpack[...] = onehot(placed)
    step_row[...] = jnp.sum(jnp.where(placed, steps_col, 0.0), axis=0, keepdims=True)
    counts = jnp.zeros((n_cells + 4 * rim, n_cells), f32)
    entry = iota((n_cells + 4 * rim, n_cells), 0)
    for face in range(4):
        counts = counts + jnp.where(adj_ref[face:face + 1, :] == entry, 1.0, 0.0)
    counts = counts.astype(bf16)

    for g in range(groups):
        part = rows_of(g)
        each_of(g, lambda b: state_copy(b).wait_recv())
        g_high, g_low = split(recv[part, :])
        into = unpack[part, :]
        more = mm(g_high, into, TN) + mm(g_low, into, TN)
        rim_more = mm(into[:, :128], g_high, TN) + mm(into[:, :128], g_low, TN)
        more = more.reshape(n_scalar, n_bins, n_cells)
        if g == 0:
            q1[...] = more
            rim_sum[...] = rim_more
        elif g < groups - 1:
            q1[...] += more
            rim_sum[...] += rim_more
        else:
            halo_out[...] = (rim_sum[...] + rim_more)[:rim]
            q1[...] += more

    beside = (
        (gx < n_gx - 1, (gx + 1, yz), 0, gx > 0),
        (gx > 0, (gx - 1, yz), 1, gx < n_gx - 1),
        (yz < n_yz - 1, (gx, yz + 1), 2, yz > 0),
        (yz > 0, (gx, yz - 1), 3, yz < n_yz - 1),
    )

    def halo_copy(dev, place):
        return pltpu.make_async_remote_copy(
            halo_out, halo_in.at[pl.ds(place * rim, rim)], h_send.at[place], h_recv.at[place],
            device_id=dev, device_id_type=mesh_id)

    for there, dev, place, _ in beside:
        @pl.when(there)
        def _start():
            halo_copy(dev, place).start()

    home_state = q1[...].reshape(rows, n_cells)
    o_high, o_low = split(home_state)
    own_counts = counts[:n_cells]
    moved = home_state * (1.0 - 4.0 * tau_face) + tau_face * (
        mm(o_high, own_counts, NN) + mm(o_low, own_counts, NN))
    for _, dev, place, from_there in beside:
        @pl.when(from_there)
        def _wait():
            halo_copy(dev, place).wait_recv()
    r_high, r_low = split(halo_in[...])
    far_counts = counts[n_cells:]
    moved = moved + tau_face * (mm(r_high, far_counts, TN) + mm(r_low, far_counts, TN))
    q0[...] = moved.reshape(n_scalar, n_bins, n_cells)

    count = step_row[...]
    size = 1.0 / jnp.maximum(count, 1.0)
    bins_at = iota((n_bins, n_cells), 0)
    first, last = bins_at == 0, bins_at == n_bins - 1

    def substep(src, dst, s):
        h = jnp.where(s.astype(f32) < count, size, 0.0)
        rate = ratio[:n_bins, :] * h
        for j in range(n_scalar):
            mixed = coup_ref[j, 0] * src[0]
            for k in range(1, n_scalar):
                mixed = mixed + coup_ref[j, k] * src[k]
            q = src[j]
            below = jnp.where(first, q, pltpu.roll(q, 1, 0))
            above = jnp.where(last, q, pltpu.roll(q, n_bins - 1, 0))
            dst[j] = q + rate * (above - 2.0 * q + below) + h * jnp.tanh(mixed)

    def pair(i, carry):
        substep(q0, q1, 2 * i)
        substep(q1, q0, 2 * i + 1)
        return carry

    lax.fori_loop(0, submax // 2, pair, 0)

    n_high, n_low = split(q0[...].reshape(rows, n_cells))
    new_high[...] = n_high
    new_low[...] = n_low
    for g in range(groups):
        part = rows_of(g)
        reply[part, :] = mm(unpack[part, :], n_high, NT) + mm(unpack[part, :], n_low, NT)
        each_of(g, lambda b: back_copy(b).start())
    back[mine, :] = reply[mine, :]

    def species_part(i, carry):
        part = pl.ds(pl.multiple_of(i * chunk, chunk), chunk)
        member = onehot(iota((n_cells, chunk), 0) == map_ref[:, part])
        w = weights[:, part]
        picked = mm(new_high[...], member, NN) + mm(new_low[...], member, NN)
        for k in range(n_scalar):
            species_ref[k:k + 1, part] = jnp.sum(
                picked[k * n_bins:(k + 1) * n_bins] * w, axis=0, keepdims=True)
        return carry

    lax.fori_loop(0, n_les // chunk, species_part, 0)

    def drain(b):
        info_copy(b).wait_send()
        state_copy(b).wait_send()

    each(drain)
    for there, dev, place, _ in beside:
        @pl.when(there)
        def _drain():
            halo_copy(dev, place).wait_send()

    for g in range(groups):
        part = rows_of(g)
        each_of(g, lambda b: back_copy(b).wait_send())
        each_of(g, lambda b: back_copy(b).wait_recv())
        b_high, b_low = split(back[part, :])
        more = (mm(b_high, pack[part, :], TN) + mm(b_low, pack[part, :], TN)).reshape(
            n_scalar, n_bins, n_cells)
        if g == 0:
            cond_ref[...] = more
        else:
            cond_ref[...] += more


def shards(n_gx, n_yz, mean_mix, segregation, dissipation, les_map, cond_state, slot_cell,
           adjacency, substeps, coupling):
    n_scalar, n_bins, n_cells = cond_state.shape
    n_les = mean_mix.shape[0]
    n = n_gx * n_yz
    rows = n_scalar * n_bins
    cap = 2 * n_cells // n
    capp = -(-cap // 8) * 8
    slots = n * capp
    rim = n_cells // 8
    chunk = min(512, n_les)
    vmem = pl.BlockSpec(memory_space=pltpu.VMEM)
    dma = pltpu.SemaphoreType.DMA
    return pl.pallas_call(
        functools.partial(kernel, n_gx, n_yz, cap, chunk),
        out_shape=(
            jax.ShapeDtypeStruct((n_scalar, n_les), f32),
            jax.ShapeDtypeStruct((n_scalar, n_bins, n_cells), f32),
        ),
        in_specs=[pl.BlockSpec(memory_space=pltpu.HBM)] * 9,
        out_specs=(vmem, vmem),
        scratch_shapes=[
            pltpu.VMEM((1, n_les), f32),
            pltpu.VMEM((1, n_les), f32),
            pltpu.VMEM((1, n_les), f32),
            pltpu.VMEM((1, n_les), jnp.int32),
            pltpu.VMEM((n_scalar, n_bins, n_cells), f32),
            pltpu.VMEM((1, n_cells), jnp.int32),
            pltpu.VMEM((4, n_cells), jnp.int32),
            pltpu.VMEM((1, n_cells), jnp.int32),
            pltpu.SMEM(coupling.shape, f32),
            pltpu.VMEM((slots, rows), f32),
            pltpu.VMEM((slots, rows), f32),
            pltpu.VMEM((slots, rows), f32),
            pltpu.VMEM((slots, rows), f32),
            pltpu.VMEM((n, 1, 128), f32),
            pltpu.VMEM((n, 1, 128), f32),
            pltpu.VMEM((n, 128), f32),
            pltpu.VMEM((rim, rows), f32),
            pltpu.VMEM((4 * rim, rows), f32),
            pltpu.VMEM((n_bins, n_les), f32),
            pltpu.VMEM((2 * n_bins, n_cells), f32),
            pltpu.VMEM((slots, n_cells), bf16),
            pltpu.VMEM((slots, n_cells), bf16),
            pltpu.VMEM((n_scalar, n_bins, n_cells), f32),
            pltpu.VMEM((n_scalar, n_bins, n_cells), f32),
            pltpu.VMEM((rows, n_cells), bf16),
            pltpu.VMEM((rows, n_cells), bf16),
            pltpu.VMEM((1, n_cells), f32),
            pltpu.VMEM((128, rows), f32),
            dma((9,)), dma((n,)), dma((n,)), dma((n,)), dma((n,)), dma((n,)), dma((n,)), dma((4,)), dma((4,)),
        ],
        compiler_params=pltpu.CompilerParams(
            collective_id=0, has_side_effects=True, vmem_limit_bytes=64 * 1024 * 1024),
        cost_estimate=pl.CostEstimate(
            flops=8 * rows * n_les * n_cells, bytes_accessed=4 * rows * n_cells,
            transcendentals=n_bins * n_les),
    )(
        mean_mix.reshape(1, n_les), segregation.reshape(1, n_les), dissipation.reshape(1, n_les),
        les_map.reshape(1, n_les), cond_state, slot_cell.reshape(1, n_cells), adjacency,
        substeps.reshape(1, n_cells), coupling,
    )


def solution(mesh):
    both = P(("gx", "yz"))
    placed = (both, both, both, both, P(None, None, ("gx", "yz")), both,
              P(None, ("gx", "yz")), both, P())
    return jax.shard_map(
        functools.partial(shards, mesh.shape["gx"], mesh.shape["yz"]),
        mesh=mesh,
        in_specs=placed,
        out_specs=(P(None, ("gx", "yz")), P(None, None, ("gx", "yz"))),
        check_vma=False,
    )
```

```python
import functools

import jax
import jax.numpy as jnp
from jax import lax
from jax.experimental import pallas as pl
from jax.experimental.pallas import tpu as pltpu
from jax.sharding import PartitionSpec as P

tau_face = 0.12
floor_mass = 0.25
submax = 8
f32, bf16 = jnp.float32, jnp.bfloat16
NN = (((1,), (0,)), ((), ()))
NT = (((1,), (1,)), ((), ()))
TN = (((0,), (0,)), ((), ()))


def split(x):
    high = x.astype(bf16)
    low = (x - high.astype(f32)).astype(bf16)
    return high, low


def mm(a, b, dims):
    return lax.dot_general(a, b, dims, preferred_element_type=f32)


def iota(shape, dim):
    return lax.broadcasted_iota(jnp.int32, shape, dim)


def onehot(mask):
    return jnp.where(mask, 1.0, 0.0).astype(bf16)


def kernel(
    n_gx, n_yz, cap, chunk,
    mean_hbm, seg_hbm, diss_hbm, map_hbm, state_hbm, slot_hbm, adj_hbm, steps_hbm, coup_hbm,
    species_ref, cond_ref,
    mean_ref, seg_ref, diss_ref, map_ref, state_ref, slot_ref, adj_ref, steps_ref, coup_ref,
    send, recv, reply, back, info_out, info_in, info_rows, halo_out, halo_in,
    weights, ratio, pack, unpack, q0, q1, new_high, new_low, step_row, rim_sum,
    a_sem,    s_send, s_recv, i_send, i_recv, b_send, b_recv, h_send, h_recv,
):
    n_scalar, n_bins, n_cells = state_ref.shape
    rows = n_scalar * n_bins
    n_les = mean_ref.shape[1]
    n = n_gx * n_yz
    slots = send.shape[0]
    capp = slots // n
    rim = halo_out.shape[0]
    gx, yz = lax.axis_index("gx"), lax.axis_index("yz")
    mesh_id = pl.DeviceIdType.MESH
    half = n_gx // 2
    groups = n_gx
    width = slots // groups

    def wrap(a, size):
        a = jnp.where(a >= size, a - size, a)
        return jnp.where(a < 0, a + size, a)

    def dg_of(i):
        odd = i - 2 * (i // 2)
        return half + (1 - 2 * odd) * ((i + 1) // 2)

    def ahead(b):
        i, j = b
        return wrap(gx + dg_of(i), n_gx), wrap(yz + (n_yz - 1 - j), n_yz)

    def behind(b):
        i, j = b
        return wrap(gx - dg_of(i), n_gx), wrap(yz - (n_yz - 1 - j), n_yz)

    def number(b):
        return b[0] * n_yz + b[1]

    def block(ref, b):
        return ref.at[pl.ds(pl.multiple_of(number(b) * capp, 8), capp)]

    def info_copy(b):
        m = number(b)
        return pltpu.make_async_remote_copy(
            info_out.at[m], info_in.at[m], i_send.at[m], i_recv.at[m],
            device_id=ahead(b), device_id_type=mesh_id)

    def state_copy(b):
        m = number(b)
        return pltpu.make_async_remote_copy(
            block(send, b), block(recv, b), s_send.at[m], s_recv.at[m],
            device_id=ahead(b), device_id_type=mesh_id)

    def back_copy(b):
        m = number(b)
        return pltpu.make_async_remote_copy(
            block(reply, b), block(back, b), b_send.at[m], b_recv.at[m],
            device_id=behind(b), device_id_type=mesh_id)

    def each(body, low=0, high=n_gx):
        def run(i, carry):
            for j in range(n_yz):
                body((i, j))
            return carry
        lax.fori_loop(low, min(high, n_gx - 1), run, 0)
        if high == n_gx:
            for j in range(n_yz - 1):
                body((n_gx - 1, j))

    def each_of(group, body):
        each(body, group * (n_gx // groups), (group + 1) * (n_gx // groups))

    def rows_of(group):
        return pl.ds(group * width, width)

    fetches = [
        pltpu.make_async_copy(src, dst, a_sem.at[i])
        for i, (src, dst) in enumerate((
            (slot_hbm, slot_ref), (steps_hbm, steps_ref), (state_hbm, state_ref),
            (mean_hbm, mean_ref), (seg_hbm, seg_ref), (diss_hbm, diss_ref),
            (map_hbm, map_ref), (adj_hbm, adj_ref), (coup_hbm, coup_ref)))
    ]
    for fetch in fetches:
        fetch.start()

    halo_in[...] = jnp.zeros_like(halo_in)
    barrier = pltpu.get_barrier_semaphore()

    def greet(b):
        pl.semaphore_signal(barrier, inc=1, device_id=ahead(b), device_id_type=mesh_id)

    each(greet)

    fetches[0].wait()
    fetches[1].wait()
    slot = slot_ref[...]
    tile = slot // n_cells
    local = slot - tile * n_cells
    tile_g = tile // n_yz
    from_half = lax.rem(tile_g - gx + n_gx, n_gx) - half
    step_i = jnp.where(from_half >= 0, 2 * from_half, -2 * from_half - 1)
    home = step_i * n_yz + n_yz - 1 - lax.rem(tile - tile_g * n_yz - yz + n_yz, n_yz)
    marks = iota((n, n_cells), 0) == home
    before = onehot(iota((n_cells, n_cells), 0) < iota((n_cells, n_cells), 1))
    earlier = mm(onehot(marks), before, NN)
    marks_f = jnp.where(marks, 1.0, 0.0)
    position = jnp.sum(earlier * marks_f, axis=0, keepdims=True).astype(jnp.int32)
    send_pos = home * capp + position
    pack[...] = onehot(iota((slots, n_cells), 0) == send_pos)

    lane = iota((128, n_cells), 0)
    at_low = onehot(lane == position)
    at_high = onehot(lane - 64 == position)
    index_part = (marks_f * (local + 1).astype(f32)).astype(bf16)
    steps_part = (marks_f * steps_ref[...].astype(f32)).astype(bf16)
    info = mm(index_part, at_low, NT) + mm(steps_part, at_high, NT)
    for d in range(n):
        info_out[d] = info[d:d + 1, :]

    fetches[2].wait()
    high, low = split(state_ref[...].reshape(rows, n_cells))
    send[rows_of(0), :] = mm(pack[rows_of(0), :], high, NT) + mm(pack[rows_of(0), :], low, NT)
    pl.semaphore_wait(barrier, n - 1)
    each_of(0, lambda b: state_copy(b).start())
    each(lambda b: info_copy(b).start())
    for g in range(1, groups):
        part = rows_of(g)
        send[part, :] = mm(pack[part, :], high, NT) + mm(pack[part, :], low, NT)
        each_of(g, lambda b: state_copy(b).start())
    info_in[n - 1] = info_out[n - 1]
    mine = pl.ds(slots - capp, capp)
    recv[mine, :] = send[mine, :]
    for fetch in fetches[3:]:
        fetch.wait()

    centre = (iota((n_bins, 128), 0).astype(f32) + 0.5) / n_bins
    log_low = jnp.log(centre)[:, :1]
    log_high = jnp.log(1.0 - centre)[:, :1]
    ratio[...] = jnp.zeros_like(ratio)

    def les_part(i, carry):
        part = pl.ds(pl.multiple_of(i * chunk, chunk), chunk)
        mean = mean_ref[:, part]
        shape_sum = 1.0 / seg_ref[:, part] - 1.0
        shape_low = mean * shape_sum
        shape_high = (1.0 - mean) * shape_sum
        density = jnp.exp((shape_low - 1.0) * log_low + (shape_high - 1.0) * log_high)
        w = density / jnp.sum(density, axis=0, keepdims=True)
        weights[:, part] = w
        moments = jnp.concatenate([w, diss_ref[:, part] * w], axis=0)
        m_high, m_low = split(moments)
        member = onehot(iota((n_cells, chunk), 0) == map_ref[:, part])
        ratio[...] += mm(m_high, member, NT) + mm(m_low, member, NT)
        return carry

    lax.fori_loop(0, n_les // chunk, les_part, 0)
    ratio[:n_bins, :] = ratio[n_bins:, :] / jnp.maximum(ratio[:n_bins, :], floor_mass)

    each(lambda b: info_copy(b).wait_recv())
    for d in range(n):
        info_rows[d:d + 1, :] = info_in[d]
    table = info_rows[...].astype(bf16)
    spread = onehot(iota((slots, n), 0) // capp == iota((slots, n), 1))
    wide = mm(spread, table, NN)
    slot_in = lax.rem(iota((slots, 128), 0), capp)
    lanes = iota((slots, 128), 1)
    index_col = jnp.sum(jnp.where(lanes == slot_in, wide, 0.0), axis=1, keepdims=True)
    steps_col = jnp.sum(jnp.where(lanes == slot_in + 64, wide, 0.0), axis=1, keepdims=True)
    placed = index_col.astype(jnp.int32) == iota((slots, n_cells), 1) + 1
    unpack[...] = onehot(placed)
    step_row[...] = jnp.sum(jnp.where(placed, steps_col, 0.0), axis=0, keepdims=True)
    counts = jnp.zeros((n_cells + 4 * rim, n_cells), f32)
    entry = iota((n_cells + 4 * rim, n_cells), 0)
    for face in range(4):
        counts = counts + jnp.where(adj_ref[face:face + 1, :] == entry, 1.0, 0.0)
    counts = counts.astype(bf16)

    for g in range(groups):
        part = rows_of(g)
        each_of(g, lambda b: state_copy(b).wait_recv())
        g_high, g_low = split(recv[part, :])
        into = unpack[part, :]
        more = mm(g_high, into, TN) + mm(g_low, into, TN)
        rim_more = mm(into[:, :128], g_high, TN) + mm(into[:, :128], g_low, TN)
        more = more.reshape(n_scalar, n_bins, n_cells)
        if g == 0:
            q1[...] = more
            rim_sum[...] = rim_more
        elif g < groups - 1:
            q1[...] += more
            rim_sum[...] += rim_more
        else:
            halo_out[...] = (rim_sum[...] + rim_more)[:rim]
            q1[...] += more

    beside = (
        (gx < n_gx - 1, (gx + 1, yz), 0, gx > 0),
        (gx > 0, (gx - 1, yz), 1, gx < n_gx - 1),
        (yz < n_yz - 1, (gx, yz + 1), 2, yz > 0),
        (yz > 0, (gx, yz - 1), 3, yz < n_yz - 1),
    )

    def halo_copy(dev, place):
        return pltpu.make_async_remote_copy(
            halo_out, halo_in.at[pl.ds(place * rim, rim)], h_send.at[place], h_recv.at[place],
            device_id=dev, device_id_type=mesh_id)

    for there, dev, place, _ in beside:
        @pl.when(there)
        def _start():
            halo_copy(dev, place).start()

    home_state = q1[...].reshape(rows, n_cells)
    o_high, o_low = split(home_state)
    own_counts = counts[:n_cells]
    moved = home_state * (1.0 - 4.0 * tau_face) + tau_face * (
        mm(o_high, own_counts, NN) + mm(o_low, own_counts, NN))
    for _, dev, place, from_there in beside:
        @pl.when(from_there)
        def _wait():
            halo_copy(dev, place).wait_recv()
    r_high, r_low = split(halo_in[...])
    far_counts = counts[n_cells:]
    moved = moved + tau_face * (mm(r_high, far_counts, TN) + mm(r_low, far_counts, TN))
    q0[...] = moved.reshape(n_scalar, n_bins, n_cells)

    count = step_row[...]
    size = 1.0 / jnp.maximum(count, 1.0)
    bins_at = iota((n_bins, n_cells), 0)
    first, last = bins_at == 0, bins_at == n_bins - 1

    def substep(src, dst, s):
        h = jnp.where(s.astype(f32) < count, size, 0.0)
        rate = ratio[:n_bins, :] * h
        for j in range(n_scalar):
            mixed = coup_ref[j, 0] * src[0]
            for k in range(1, n_scalar):
                mixed = mixed + coup_ref[j, k] * src[k]
            q = src[j]
            below = jnp.where(first, q, pltpu.roll(q, 1, 0))
            above = jnp.where(last, q, pltpu.roll(q, n_bins - 1, 0))
            dst[j] = q + rate * (above - 2.0 * q + below) + h * jnp.tanh(mixed)

    def pair(i, carry):
        substep(q0, q1, 2 * i)
        substep(q1, q0, 2 * i + 1)
        return carry

    lax.fori_loop(0, submax // 2, pair, 0)

    n_high, n_low = split(q0[...].reshape(rows, n_cells))
    new_high[...] = n_high
    new_low[...] = n_low
    for g in range(groups):
        part = rows_of(g)
        reply[part, :] = mm(unpack[part, :], n_high, NT) + mm(unpack[part, :], n_low, NT)
        each_of(g, lambda b: back_copy(b).start())
    back[mine, :] = reply[mine, :]

    def species_part(i, carry):
        part = pl.ds(pl.multiple_of(i * chunk, chunk), chunk)
        member = onehot(iota((n_cells, chunk), 0) == map_ref[:, part])
        w = weights[:, part]
        picked = mm(new_high[...], member, NN) + mm(new_low[...], member, NN)
        for k in range(n_scalar):
            species_ref[k:k + 1, part] = jnp.sum(
                picked[k * n_bins:(k + 1) * n_bins] * w, axis=0, keepdims=True)
        return carry

    lax.fori_loop(0, n_les // chunk, species_part, 0)

    def drain(b):
        info_copy(b).wait_send()
        state_copy(b).wait_send()

    each(drain)
    for there, dev, place, _ in beside:
        @pl.when(there)
        def _drain():
            halo_copy(dev, place).wait_send()

    for g in range(groups):
        part = rows_of(g)
        each_of(g, lambda b: back_copy(b).wait_send())
        each_of(g, lambda b: back_copy(b).wait_recv())
        b_high, b_low = split(back[part, :])
        more = (mm(b_high, pack[part, :], TN) + mm(b_low, pack[part, :], TN)).reshape(
            n_scalar, n_bins, n_cells)
        if g == 0:
            cond_ref[...] = more
        else:
            cond_ref[...] += more


def shards(n_gx, n_yz, mean_mix, segregation, dissipation, les_map, cond_state, slot_cell,
           adjacency, substeps, coupling):
    n_scalar, n_bins, n_cells = cond_state.shape
    n_les = mean_mix.shape[0]
    n = n_gx * n_yz
    rows = n_scalar * n_bins
    cap = 2 * n_cells // n
    capp = -(-cap // 8) * 8
    slots = n * capp
    rim = n_cells // 8
    chunk = min(512, n_les)
    vmem = pl.BlockSpec(memory_space=pltpu.VMEM)
    dma = pltpu.SemaphoreType.DMA
    return pl.pallas_call(
        functools.partial(kernel, n_gx, n_yz, cap, chunk),
        out_shape=(
            jax.ShapeDtypeStruct((n_scalar, n_les), f32),
            jax.ShapeDtypeStruct((n_scalar, n_bins, n_cells), f32),
        ),
        in_specs=[pl.BlockSpec(memory_space=pltpu.HBM)] * 9,
        out_specs=(vmem, vmem),
        scratch_shapes=[
            pltpu.VMEM((1, n_les), f32),
            pltpu.VMEM((1, n_les), f32),
            pltpu.VMEM((1, n_les), f32),
            pltpu.VMEM((1, n_les), jnp.int32),
            pltpu.VMEM((n_scalar, n_bins, n_cells), f32),
            pltpu.VMEM((1, n_cells), jnp.int32),
            pltpu.VMEM((4, n_cells), jnp.int32),
            pltpu.VMEM((1, n_cells), jnp.int32),
            pltpu.SMEM(coupling.shape, f32),
            pltpu.VMEM((slots, rows), f32),
            pltpu.VMEM((slots, rows), f32),
            pltpu.VMEM((slots, rows), f32),
            pltpu.VMEM((slots, rows), f32),
            pltpu.VMEM((n, 1, 128), f32),
            pltpu.VMEM((n, 1, 128), f32),
            pltpu.VMEM((n, 128), f32),
            pltpu.VMEM((rim, rows), f32),
            pltpu.VMEM((4 * rim, rows), f32),
            pltpu.VMEM((n_bins, n_les), f32),
            pltpu.VMEM((2 * n_bins, n_cells), f32),
            pltpu.VMEM((slots, n_cells), bf16),
            pltpu.VMEM((slots, n_cells), bf16),
            pltpu.VMEM((n_scalar, n_bins, n_cells), f32),
            pltpu.VMEM((n_scalar, n_bins, n_cells), f32),
            pltpu.VMEM((rows, n_cells), bf16),
            pltpu.VMEM((rows, n_cells), bf16),
            pltpu.VMEM((1, n_cells), f32),
            pltpu.VMEM((128, rows), f32),
            dma((9,)), dma((n,)), dma((n,)), dma((n,)), dma((n,)), dma((n,)), dma((n,)), dma((4,)), dma((4,)),
        ],
        compiler_params=pltpu.CompilerParams(
            collective_id=0, has_side_effects=True, vmem_limit_bytes=64 * 1024 * 1024),
        cost_estimate=pl.CostEstimate(
            flops=8 * rows * n_les * n_cells, bytes_accessed=4 * rows * n_cells,
            transcendentals=n_bins * n_les),
    )(
        mean_mix.reshape(1, n_les), segregation.reshape(1, n_les), dissipation.reshape(1, n_les),
        les_map.reshape(1, n_les), cond_state, slot_cell.reshape(1, n_cells), adjacency,
        substeps.reshape(1, n_cells), coupling,
    )


def solution(mesh):
    both = P(("gx", "yz"))
    placed = (both, both, both, both, P(None, None, ("gx", "yz")), both,
              P(None, ("gx", "yz")), both, P())
    return jax.shard_map(
        functools.partial(shards, mesh.shape["gx"], mesh.shape["yz"]),
        mesh=mesh,
        in_specs=placed,
        out_specs=(P(None, ("gx", "yz")), P(None, None, ("gx", "yz"))),
        check_vma=False,
    )
```
